32 devices in a mesh: curve: 8 (over y, x, core), sub: 4 (over z).
Axes of the slice: x: 2, y: 2, z: 4, core: 2. Of those that a mesh axis runs over, the one named last changes fastest.
Arguments:
- fields: float32 [96, 5, 16, 256], P(('curve', 'sub'))
- new_source: int32 [96], replicated, may hold values from -1 to 95, as said below
- ghost_source: int32 [96, 6], replicated, may hold values from -1 to 95, as said below
Outputs:
- advanced_fields: float32 [96, 5, 16, 256], P(('curve', 'sub'))
The draws below stay inside these ranges and needn't reach their ends.
Inputs may be any that keep to these rules, and one draw needn't show every extreme that they name: `new_source`: entry j names the slot whose box slot j holds after the regrid, or -1 where slot j is empty. Slots are numbered segment by segment along the curve (3 a segment). The named slot lies on the same curve segment or on one next to it (the curve does not close), no slot is named twice, every segment holds at least one box, and at most one box goes from one segment to one neighbouring segment, exactly one for some pair. `ghost_source`: entries are -1 exactly for the faces of empty slots (new_source -1); every other entry names an occupied slot on a curve segment at most 2 away along the curve, which here closes on itself. The faces of one segment draw on one segment, itself included, at most 4 times, exactly 4 times for some pair.
All inputs are finite; a program needn't handle non-finite values.
Results may differ from the reference program's by a relative error of at most 0.0003.
Values sent between devices are 32-bit elements; how exact they have to be, the bound alone decides.
A program may use at most 64 MiB of HBM per device.

```python
import math
import jax
import jax.numpy as jnp
from jax import lax

BX = 16
SLOTS = 3
GHOST = 2
MOVE = 1
REACH = 2
NB = 96


GAMMA = 5.0 / 3.0


def box_lists(key):
    segments = NB // SLOTS
    stay_count = SLOTS - 2 * MOVE
    key_list = jax.random.split(key, 8)
    old_order = jax.vmap(lambda sub_key: jax.random.permutation(sub_key, SLOTS))(jax.random.split(key_list[0], segments))
    new_order = jax.vmap(lambda sub_key: jax.random.permutation(sub_key, SLOTS))(jax.random.split(key_list[1], segments))
    from_left = jax.random.randint(key_list[2], (segments,), 0, MOVE + 1)
    from_right = jax.random.randint(key_list[3], (segments,), 0, MOVE + 1)
    staying = jax.random.randint(key_list[4], (segments,), 1, stay_count + 1)
    from_left = from_left.at[0].set(0).at[1].set(MOVE)
    from_right = from_right.at[segments - 1].set(0).at[1].set(MOVE)
    staying = staying.at[1].set(stay_count)
    device = jnp.arange(segments, dtype=jnp.int32)
    slot_index = jnp.broadcast_to(jnp.arange(SLOTS, dtype=jnp.int32)[None, :], (segments, SLOTS))
    left_dev = jnp.maximum(device - 1, 0)
    right_dev = jnp.minimum(device + 1, segments - 1)
    lower = from_left[:, None]
    middle = staying[:, None]
    upper = from_right[:, None]
    left_pick = left_dev[:, None] * SLOTS + jnp.take_along_axis(old_order[left_dev], MOVE + jnp.clip(slot_index, 0, MOVE - 1), axis=1)
    stay_pick = device[:, None] * SLOTS + jnp.take_along_axis(old_order, 2 * MOVE + jnp.clip(slot_index - lower, 0, stay_count - 1), axis=1)
    right_pick = right_dev[:, None] * SLOTS + jnp.take_along_axis(old_order[right_dev], jnp.clip(slot_index - lower - middle, 0, MOVE - 1), axis=1)
    candidate = jnp.where(slot_index < lower, left_pick, jnp.where(slot_index < lower + middle, stay_pick, jnp.where(slot_index < lower + middle + upper, right_pick, -1)))
    inverse = jnp.argsort(new_order, axis=1)
    new_source = jnp.take_along_axis(candidate, inverse, axis=1)
    occupied = new_source >= 0
    held_count = from_left + staying + from_right
    occupied_slots = jnp.argsort(jnp.where(occupied, slot_index, SLOTS + slot_index), axis=1)
    entries = 6 * SLOTS
    spread = jax.vmap(lambda sub_key: jax.random.permutation(sub_key, entries))(jax.random.split(key_list[5], segments))
    rotation = jax.random.randint(key_list[6], (segments, 1), 0, 2 * REACH + 1)
    offset = (spread + rotation) % (2 * REACH + 1) - REACH
    source_dev = (device[:, None] - offset) % segments
    raw_pick = jax.random.randint(key_list[7], (segments, entries), 0, 7 * SLOTS)
    pick_index = raw_pick % held_count[source_dev]
    source_slot = occupied_slots[source_dev, pick_index]
    entry_slot = jnp.broadcast_to((jnp.arange(entries, dtype=jnp.int32) // 6)[None, :], (segments, entries))
    is_valid = jnp.take_along_axis(occupied, entry_slot, axis=1)
    ghost_list = jnp.where(is_valid, source_dev * SLOTS + source_slot, -1)
    return (new_source.reshape(NB).astype(jnp.int32), ghost_list.reshape(NB, 6).astype(jnp.int32))


def draw_new_source(key, part):
    return box_lists(key)[0]


def draw_ghost_source(key, part):
    return box_lists(key)[1]


def draw_fields(key, part):
    key = jax.random.fold_in(key, 5)
    sub_keys = jax.random.split(key, 4)
    grid_shape = (NB, BX, BX * BX)
    density = jnp.exp(jax.random.uniform(sub_keys[0], grid_shape, jnp.float32, math.log(0.5), math.log(2.0)))
    pressure = jnp.exp(jax.random.uniform(sub_keys[1], grid_shape, jnp.float32, math.log(0.5), math.log(2.0)))
    box_scale = jnp.exp(jax.random.uniform(sub_keys[2], (NB, 1, 1), jnp.float32, math.log(0.3), math.log(2.0)))
    velocity = jnp.clip(jax.random.normal(sub_keys[3], (3,) + grid_shape, jnp.float32), -2.5, 2.5) * box_scale
    energy = pressure / (GAMMA - 1.0) + 0.5 * density * (velocity[0] * velocity[0] + velocity[1] * velocity[1] + velocity[2] * velocity[2])
    return jnp.stack([density, density * velocity[0], density * velocity[1], density * velocity[2], energy], axis=1).astype(jnp.float32)


def setup_inputs(seed: int = 0) -> dict:
    arg_keys = jax.random.split(jax.random.key(seed), 4)
    return {
        "fields": draw_fields(jax.random.fold_in(arg_keys[3], 71), 0),
        "new_source": draw_new_source(jax.random.fold_in(arg_keys[3], 71), 0),
        "ghost_source": draw_ghost_source(jax.random.fold_in(arg_keys[3], 71), 0),
    }


GAMMA = 5.0 / 3.0
COURANT = 0.3
FILLER = (1.0, 0.0, 0.0, 0.0, 1.5)

def filler(trailing):
    return jnp.array(FILLER, jnp.float32).reshape((5,) + (1,) * trailing)

def minmod(lower_step, upper_step):
    return 0.5 * (jnp.sign(lower_step) + jnp.sign(upper_step)) * jnp.minimum(jnp.abs(lower_step), jnp.abs(upper_step))

def primitives(state):
    density = state[:, 0]
    vel_x = state[:, 1] / density
    vel_y = state[:, 2] / density
    vel_z = state[:, 3] / density
    kinetic = 0.5 * density * (vel_x * vel_x + vel_y * vel_y + vel_z * vel_z)
    pressure = (GAMMA - 1.0) * (state[:, 4] - kinetic)
    return [density, vel_x, vel_y, vel_z, pressure]

def euler_terms(primitive, normal):
    density, vel_x, vel_y, vel_z, pressure = primitive
    along = primitive[normal]
    energy = pressure / (GAMMA - 1.0) + 0.5 * density * (vel_x * vel_x + vel_y * vel_y + vel_z * vel_z)
    conserved = [density, density * vel_x, density * vel_y, density * vel_z, energy]
    fluxes = [value * along for value in conserved]
    fluxes[normal] = fluxes[normal] + pressure
    fluxes[4] = fluxes[4] + pressure * along
    speeds = jnp.abs(along) + jnp.sqrt(GAMMA * pressure / density)
    return (conserved, fluxes, speeds)

def flux_sweep(primitive, axis_index, normal):
    interior = primitive[0].shape[axis_index] - 4

    def cut_range(array_in, start_at, stop_at):
        return lax.slice_in_dim(array_in, start_at, stop_at, axis=axis_index)
    lefts = []
    rights = []
    for values in primitive:
        steps = cut_range(values, 1, interior + 4) - cut_range(values, 0, interior + 3)
        slope = minmod(cut_range(steps, 0, interior + 2), cut_range(steps, 1, interior + 3))
        lefts.append(cut_range(values, 1, interior + 2) + 0.5 * cut_range(slope, 0, interior + 1))
        rights.append(cut_range(values, 2, interior + 3) - 0.5 * cut_range(slope, 1, interior + 2))
    cons_left, flux_left, speed_left = euler_terms(lefts, normal)
    cons_right, flux_right, speed_right = euler_terms(rights, normal)
    wave_speed = jnp.maximum(speed_left, speed_right)
    differences = []
    for field_index in range(5):
        face_flux = 0.5 * (flux_left[field_index] + flux_right[field_index]) - 0.5 * wave_speed * (cons_right[field_index] - cons_left[field_index])
        differences.append(cut_range(face_flux, 1, interior + 1) - cut_range(face_flux, 0, interior))
    return jnp.stack(differences, axis=1)

def side_strips(box_cells):
    box_edge = box_cells.shape[-1]
    low_x = jnp.swapaxes(box_cells[..., :GHOST], -1, -2)
    high_x = jnp.swapaxes(box_cells[..., box_edge - GHOST:], -1, -2)
    low_y = box_cells[..., :GHOST, :]
    high_y = box_cells[..., box_edge - GHOST:, :]
    low_z = jnp.swapaxes(box_cells[:, :, :GHOST], 2, 3)
    high_z = jnp.swapaxes(box_cells[:, :, box_edge - GHOST:], 2, 3)
    return jnp.stack([low_x, high_x, low_y, high_y, low_z, high_z], axis=1)

def fastest(box_cells, occupied):
    primitive = primitives(box_cells)
    sound = jnp.sqrt(GAMMA * primitive[4] / primitive[0])
    quickest = jnp.maximum(jnp.maximum(jnp.abs(primitive[1]), jnp.abs(primitive[2])), jnp.abs(primitive[3])) + sound
    return jnp.max(jnp.where(occupied[:, None, None, None], quickest, 0.0))

def advance(box_cells, ghosts, time_ratio, occupied):
    along_x = jnp.concatenate([jnp.swapaxes(ghosts[:, 0], -1, -2), box_cells, jnp.swapaxes(ghosts[:, 1], -1, -2)], axis=4)
    along_y = jnp.concatenate([ghosts[:, 2], box_cells, ghosts[:, 3]], axis=3)
    along_z = jnp.concatenate([jnp.swapaxes(ghosts[:, 4], 2, 3), box_cells, jnp.swapaxes(ghosts[:, 5], 2, 3)], axis=2)
    summed = flux_sweep(primitives(along_x), 3, 1) + flux_sweep(primitives(along_y), 2, 2)
    summed = summed + flux_sweep(primitives(along_z), 1, 3)
    updated = box_cells - time_ratio * summed
    return jnp.where(occupied[:, None, None, None, None], updated, 0.0)

def reference(fields, new_source, ghost_source):
    box_total, field_count, box_edge, cells = fields.shape
    segments = box_total // SLOTS
    occupied = new_source >= 0
    moved_boxes = jnp.take(fields, jnp.maximum(new_source, 0), axis=0)
    moved_boxes = jnp.where(occupied[:, None, None, None], moved_boxes, filler(2))
    box_cells = moved_boxes.reshape(box_total, field_count, box_edge, box_edge, box_edge)
    groups = box_cells.reshape(segments, SLOTS, field_count, box_edge, box_edge, box_edge)
    group_occupied = occupied.reshape(segments, SLOTS)
    speeds = lax.map(lambda group_item: fastest(group_item[0], group_item[1]), (groups, group_occupied))
    time_ratio = COURANT / jnp.max(speeds)
    strips = side_strips(box_cells).reshape(box_total * 6, field_count, box_edge, GHOST, box_edge)
    group_sources = ghost_source.reshape(segments, SLOTS, 6)

    def one_group(group_item):
        box_group, occupied_group, source_group = group_item
        wanted = jnp.maximum(source_group, 0) * 6 + jnp.array([1, 0, 3, 2, 5, 4], jnp.int32)[None, :]
        ghosts = jnp.take(strips, wanted.reshape(-1), axis=0).reshape(SLOTS, 6, field_count, box_edge, GHOST, box_edge)
        ghosts = jnp.where((source_group >= 0)[:, :, None, None, None, None], ghosts, filler(3))
        return advance(box_group, ghosts, time_ratio, occupied_group)
    result = lax.map(one_group, (groups, group_occupied, group_sources))
    return result.reshape(box_total, field_count, box_edge, cells)
```

```python
import functools

import jax
import jax.numpy as jnp
from jax import lax
from jax.experimental import pallas as pl
from jax.experimental.pallas import tpu as pltpu
from jax.sharding import PartitionSpec as P

MESH = pl.DeviceIdType.MESH
SHIFTS = (1, -1, 2, -2)
CAPG = 4
SIDES = (1, 0, 3, 2, 5, 4)
GAMMA = 5.0 / 3.0
COURANT = 0.3
FILLER = (1.0, 0.0, 0.0, 0.0, 1.5)
VMEM = pl.BlockSpec(memory_space=pltpu.VMEM)
SMEM = pl.BlockSpec(memory_space=pltpu.SMEM)


def iota(shape, dim):
    return lax.broadcasted_iota(jnp.int32, shape, dim)


def dot(a, b):
    return jnp.dot(a, b, precision=lax.Precision.HIGHEST, preferred_element_type=jnp.float32)


def repeated(value):
    value = value + pltpu.roll(value, 64, 1)
    return value + pltpu.roll(value, 32, 1)


def primitives(state):
    inverse = 1.0 / state[0]
    vel = [state[k] * inverse for k in (1, 2, 3)]
    kinetic = 0.5 * state[0] * (vel[0] * vel[0] + vel[1] * vel[1] + vel[2] * vel[2])
    return [state[0], *vel, (GAMMA - 1.0) * (state[4] - kinetic)]


def exchange_kernel(
    sizes, fields, new_source, ghost, moved, packed, top,
    strips, move_out, move_in, face_out, face_in, top_out, top_in, top_out2, top_in2,
    move_sems, face_sems, top_sems, top_sems2,
):
    curves, subs = sizes
    count = curves * subs
    slots = fields.shape[0]
    curve, sub = lax.axis_index("curve"), lax.axis_index("sub")
    here = curve * subs + sub

    def at(shift):
        other = lax.rem(here + shift + count, count)
        return (other // subs, lax.rem(other, subs))

    sub_peers = [(curve, lax.rem(sub + k, subs)) for k in range(1, subs)]
    curve_peers = [(lax.rem(curve + k, curves), sub) for k in range(1, curves)]
    barrier = pltpu.get_barrier_semaphore()
    peers = sub_peers + curve_peers + [at(s) for s in SHIFTS]
    for peer in peers:
        pl.semaphore_signal(barrier, inc=1, device_id=peer, device_id_type=MESH)

    base = here * slots
    for n, shift in enumerate((1, -1)):
        receiver = lax.rem(here + shift + count, count)
        pick = jnp.int32(0)
        for j in range(slots):
            source = new_source[receiver * slots + j] - base
            pick = jnp.where((source >= 0) & (source < slots), source, pick)
        move_out[n] = fields[pick]

    around = [
        new_source[lax.rem(here + s + count, count) * slots + j]
        for s in (-1, 0, 1)
        for j in range(slots)
    ]
    fastest = jnp.zeros((8, 128), jnp.float32)
    for b in range(slots):
        used = jnp.int32(0)
        for source in around:
            used = jnp.where(source == base + b, 1, used)
        prim = primitives([fields[b, k] for k in range(5)])
        quick = jnp.maximum(jnp.maximum(jnp.abs(prim[1]), jnp.abs(prim[2])), jnp.abs(prim[3]))
        quick = quick + jnp.sqrt(GAMMA * prim[4] / prim[0])
        quick = jnp.where(used > 0, quick, 0.0)
        for r in (0, 8):
            for c in (0, 128):
                fastest = jnp.maximum(fastest, quick[r : r + 8, c : c + 128])
    top_out[...] = fastest

    pl.semaphore_wait(barrier, len(peers))

    moves = []
    for n, shift in enumerate((1, -1)):
        moves.append(
            pltpu.make_async_remote_copy(
                move_out.at[n], move_in.at[n], move_sems.at[0, n], move_sems.at[1, n],
                device_id=at(shift), device_id_type=MESH,
            )
        )
        moves[-1].start()
    firsts = []
    for n, peer in enumerate(sub_peers):
        firsts.append(
            pltpu.make_async_remote_copy(
                top_out, top_in.at[n], top_sems.at[0, n], top_sems.at[1, n],
                device_id=peer, device_id_type=MESH,
            )
        )
        firsts[-1].start()

    picks = []
    for shift in (0,) + SHIFTS:
        receiver = lax.rem(here + shift + count, count)
        rank = jnp.int32(0)
        chosen = [jnp.int32(0)] * CAPG
        for j in range(slots):
            for f in range(6):
                source = ghost[f, receiver * slots + j] - base
                going = (source >= 0) & (source < slots)
                row = source * 6 + SIDES[f]
                for k in range(CAPG):
                    chosen[k] = jnp.where(going & (rank == k), row, chosen[k])
                rank = rank + jnp.where(going, 1, 0)
        picks.append(chosen)

    own = [new_source[base + j] for j in range(slots)]
    for copy in firsts:
        copy.wait()
    fastest = top_out[...]
    for n in range(subs - 1):
        fastest = jnp.maximum(fastest, top_in[n])
    top_out2[...] = fastest
    seconds = []
    for n, peer in enumerate(curve_peers):
        seconds.append(
            pltpu.make_async_remote_copy(
                top_out2, top_in2.at[n], top_sems2.at[0, n], top_sems2.at[1, n],
                device_id=peer, device_id_type=MESH,
            )
        )
        seconds[-1].start()

    cell, column = iota((256, 256), 0), iota((256, 256), 1)
    inside = lax.rem(column, 32)
    wanted_cell = (inside // 2) * 16 + lax.rem(inside, 2) + jnp.where(column >= 128, 14, 0)
    x_picker = jnp.where(cell == wanted_cell, 1.0, 0.0)
    lane16 = iota((16, 128), 1)
    lane8, row8 = iota((8, 128), 1), iota((8, 128), 0)
    group_here = (lane8 // 32) == lax.rem(row8, 4)

    for copy in moves:
        copy.wait()
    for j in range(slots):
        source = own[j] - base
        local = (source >= 0) & (source < slots)
        slot = jnp.where(local, source, 0)
        for k in range(5):
            value = jnp.where(source < 0, move_in[0, k], move_in[1, k])
            value = jnp.where(local, fields[slot, k], value)
            moved[j, k] = jnp.where(own[j] >= 0, value, FILLER[k])
        for k in range(5):
            box = moved[j, k]
            x_strips = dot(box, x_picker)
            strips[j * 6 + 0, k] = x_strips[:, :128]
            strips[j * 6 + 1, k] = x_strips[:, 128:]
            strips[j * 6 + 2, k] = repeated(jnp.where(lane16 < 32, box[:, :128], 0.0))
            strips[j * 6 + 3, k] = repeated(jnp.where(lane16 >= 96, box[:, 128:], 0.0))
            for side, first in ((4, 0), (5, 14)):
                for layer in range(2):
                    line = box[first + layer : first + layer + 1]
                    spread = jnp.where(
                        row8 < 4,
                        jnp.broadcast_to(line[:, :128], (8, 128)),
                        jnp.broadcast_to(line[:, 128:], (8, 128)),
                    )
                    strips[j * 6 + side, k, pl.ds(layer * 8, 8)] = repeated(
                        jnp.where(group_here, spread, 0.0)
                    )

    group = iota((5, 16, 128), 2) // 32

    def gathered(chosen):
        value = strips[chosen[0]]
        for k in range(1, CAPG):
            value = jnp.where(group == k, strips[chosen[k]], value)
        return value

    faces = []
    for n, shift in enumerate(SHIFTS):
        face_out[n] = gathered(picks[n + 1])
        faces.append(
            pltpu.make_async_remote_copy(
                face_out.at[n], face_in.at[n], face_sems.at[0, n], face_sems.at[1, n],
                device_id=at(shift), device_id_type=MESH,
            )
        )
        faces[-1].start()
    packed[0] = gathered(picks[0])
    for copy in seconds:
        copy.wait()
    fastest = top_out2[...]
    for n in range(curves - 1):
        fastest = jnp.maximum(fastest, top_in2[n])
    top[...] = fastest
    for n, copy in enumerate(faces):
        copy.wait()
        packed[n + 1] = face_in[n]


def earlier(pair, axis):
    if axis == 0:
        edge = iota((16, 256), 1) % 16 == 0
        near = [pltpu.roll(v, 1, 1) for v in pair]
        far = [pltpu.roll(v, 241, 1) for v in pair]
    elif axis == 1:
        edge = iota((16, 256), 1) < 16
        near = far = [pltpu.roll(v, 16, 1) for v in pair]
    else:
        edge = iota((16, 256), 0) == 0
        near = far = [pltpu.roll(v, 1, 0) for v in pair]
    return jnp.where(edge, far[1], near[0]), jnp.where(edge, far[0], near[1])


def later(pair, axis, both=True):
    if axis == 0:
        edge = iota((16, 256), 1) % 16 == 15
        near = [pltpu.roll(v, 255, 1) for v in pair]
        far = [pltpu.roll(v, 15, 1) for v in pair]
    elif axis == 1:
        edge = iota((16, 256), 1) >= 240
        near = far = [pltpu.roll(v, 240, 1) for v in pair]
    else:
        edge = iota((16, 256), 0) == 15
        near = far = [pltpu.roll(v, 15, 0) for v in pair]
    first = jnp.where(edge, far[1], near[0])
    if not both:
        return first
    return first, jnp.where(edge, far[0], near[1])


def euler_terms(prim, axis):
    density, vel, pressure = prim[0], prim[1:4], prim[4]
    along = vel[axis]
    energy = pressure * (1.0 / (GAMMA - 1.0)) + 0.5 * density * (
        vel[0] * vel[0] + vel[1] * vel[1] + vel[2] * vel[2]
    )
    conserved = [density, density * vel[0], density * vel[1], density * vel[2], energy]
    fluxes = [value * along for value in conserved]
    fluxes[axis + 1] = fluxes[axis + 1] + pressure
    fluxes[4] = fluxes[4] + pressure * along
    return conserved, fluxes, jnp.abs(along) + jnp.sqrt(GAMMA * pressure / density)


def face_flux(left, right, axis):
    cons_l, flux_l, speed_l = euler_terms(left, axis)
    cons_r, flux_r, speed_r = euler_terms(right, axis)
    speed = jnp.maximum(speed_l, speed_r)
    return [0.5 * (flux_l[k] + flux_r[k]) - 0.5 * speed * (cons_r[k] - cons_l[k]) for k in range(5)]


def sweep(prim, prim_ghost, axis):
    lefts, rights = ([], []), ([], [])
    for k in range(5):
        pair = (prim[k], prim_ghost[k])
        before = earlier(pair, axis)
        step = (pair[0] - before[0], pair[1] - before[1])
        after = later(step, axis)
        ends = []
        for i in range(2):
            slope = jnp.maximum(0.0, jnp.minimum(step[i], after[i])) + jnp.minimum(
                0.0, jnp.maximum(step[i], after[i])
            )
            ends.append(pair[i] + 0.5 * slope)
            rights[i].append(pair[i] - 0.5 * slope)
        before = earlier(ends, axis)
        lefts[0].append(before[0])
        lefts[1].append(before[1])
    inner = face_flux(lefts[0], rights[0], axis)
    outer = face_flux(lefts[1], rights[1], axis)
    return [later((inner[k], outer[k]), axis, False) - inner[k] for k in range(5)]


def advance_kernel(sizes, moved, packed, top, new_source, ghost, out, where_from):
    curves, subs = sizes
    count = curves * subs
    slots = moved.shape[0]
    here = lax.axis_index("curve") * subs + lax.axis_index("sub")
    base = here * slots
    ranks = [jnp.int32(0)] * 5
    for j in range(slots):
        for f in range(6):
            source = ghost[f, base + j]
            row, group = jnp.int32(0), jnp.int32(-1)
            for n, shift in enumerate((0,) + SHIFTS):
                offset = source - lax.rem(here - shift + count, count) * slots
                hit = (offset >= 0) & (offset < slots)
                row = jnp.where(hit, n, row)
                group = jnp.where(hit, ranks[n], group)
                ranks[n] = ranks[n] + jnp.where(hit, 1, 0)
            where_from[0, j * 6 + f] = row
            where_from[1, j * 6 + f] = group
    ratio = COURANT / jnp.max(top[...])
    row_in, column = iota((256, 256), 0), iota((256, 256), 1)
    x = column % 16
    low_cell = (column // 16) * 2 + x - 14
    high_cell = 128 + (column // 16) * 2 + x
    x_spread = jnp.where(
        ((x >= 14) & (row_in == low_cell)) | ((x < 2) & (row_in == high_cell)), 1.0, 0.0
    )
    lane, row16 = iota((16, 128), 1), iota((16, 128), 0)
    row_wide = iota((16, 256), 0)

    @pl.loop(0, slots)
    def _(j):
        def strip(f, k):
            group = where_from[1, j * 6 + f]
            value = packed[where_from[0, j * 6 + f], k]
            value = repeated(jnp.where(lane // 32 == group, value, 0.0))
            return jnp.where(group >= 0, value, FILLER[k])

        def z_lines(f, k):
            value = jnp.where(lane // 32 == row16 % 4, strip(f, k), 0.0)
            sums = [jnp.sum(value[4 * i : 4 * i + 4], axis=0, keepdims=True) for i in range(4)]
            return [jnp.concatenate(sums[2 * i : 2 * i + 2], axis=1) for i in range(2)]

        box = [moved[j, k] for k in range(5)]
        prim = primitives(box)
        total = None
        for axis in range(3):
            ghosts = []
            for k in range(5):
                if axis < 2:
                    low, high = strip(2 * axis, k), strip(2 * axis + 1, k)
                if axis == 0:
                    ghosts.append(dot(jnp.concatenate([low, high], axis=1), x_spread))
                elif axis == 1:
                    ghosts.append(jnp.concatenate([high, low], axis=1))
                else:
                    low, high = z_lines(4, k), z_lines(5, k)
                    value = jnp.where(row_wide == 14, low[0], low[1])
                    value = jnp.where(row_wide == 1, high[1], value)
                    ghosts.append(jnp.where(row_wide == 0, high[0], value))
            change = sweep(prim, primitives(ghosts), axis)
            total = change if total is None else [a + b for a, b in zip(total, change)]
        taken = new_source[base + j] >= 0
        for k in range(5):
            out[j, k] = jnp.where(taken, box[k] - ratio * total[k], 0.0)


def body(sizes, fields, new_source, ghost_source):
    curves, subs = sizes
    slots = fields.shape[0]
    ghost = ghost_source.T
    f32 = jnp.float32
    tile = (5, 16, 128)
    moved, packed, top = pl.pallas_call(
        functools.partial(exchange_kernel, sizes),
        out_shape=[
            jax.ShapeDtypeStruct(fields.shape, f32),
            jax.ShapeDtypeStruct((5,) + tile, f32),
            jax.ShapeDtypeStruct((8, 128), f32),
        ],
        in_specs=[VMEM, SMEM, SMEM],
        out_specs=[VMEM] * 3,
        scratch_shapes=[
            pltpu.VMEM((slots * 6,) + tile, f32),
            pltpu.VMEM((2,) + fields.shape[1:], f32),
            pltpu.VMEM((2,) + fields.shape[1:], f32),
            pltpu.VMEM((4,) + tile, f32),
            pltpu.VMEM((4,) + tile, f32),
            pltpu.VMEM((8, 128), f32),
            pltpu.VMEM((subs - 1, 8, 128), f32),
            pltpu.VMEM((8, 128), f32),
            pltpu.VMEM((curves - 1, 8, 128), f32),
            pltpu.SemaphoreType.DMA((2, 2)),
            pltpu.SemaphoreType.DMA((2, 4)),
            pltpu.SemaphoreType.DMA((2, subs - 1)),
            pltpu.SemaphoreType.DMA((2, curves - 1)),
        ],
        compiler_params=pltpu.CompilerParams(
            collective_id=0, has_side_effects=True, vmem_limit_bytes=24 << 20
        ),
    )(fields, new_source, ghost)
    return pl.pallas_call(
        functools.partial(advance_kernel, sizes),
        out_shape=jax.ShapeDtypeStruct(fields.shape, f32),
        in_specs=[VMEM, VMEM, VMEM, SMEM, SMEM],
        out_specs=VMEM,
        scratch_shapes=[pltpu.SMEM((2, slots * 6), jnp.int32)],
        compiler_params=pltpu.CompilerParams(vmem_limit_bytes=24 << 20),
    )(moved, packed, top, new_source, ghost)


def solution(mesh):
    placed = P(("curve", "sub"), None, None, None)
    sizes = (mesh.shape["curve"], mesh.shape["sub"])
    return jax.shard_map(
        functools.partial(body, sizes),
        mesh=mesh,
        in_specs=(placed, P(), P()),
        out_specs=placed,
        check_vma=False,
    )
```

```python
import functools

import jax
import jax.numpy as jnp
from jax import lax
from jax.experimental import pallas as pl
from jax.experimental.pallas import tpu as pltpu
from jax.sharding import PartitionSpec as P

MESH = pl.DeviceIdType.MESH
SHIFTS = (1, -1, 2, -2)
CAPG = 4
SIDES = (1, 0, 3, 2, 5, 4)
GAMMA = 5.0 / 3.0
COURANT = 0.3
FILLER = (1.0, 0.0, 0.0, 0.0, 1.5)
VMEM = pl.BlockSpec(memory_space=pltpu.VMEM)
SMEM = pl.BlockSpec(memory_space=pltpu.SMEM)


def iota(shape, dim):
    return lax.broadcasted_iota(jnp.int32, shape, dim)


def picked(values, one_hot):
    rows = values.shape[0]
    parts = []
    for _ in range(3):
        parts.append(values.astype(jnp.bfloat16))
        values = values - parts[-1].astype(jnp.float32)
    product = jnp.dot(jnp.concatenate(parts, axis=0), one_hot, preferred_element_type=jnp.float32)
    return product[:rows] + product[rows : 2 * rows] + product[2 * rows :]


def repeated(value):
    value = value + pltpu.roll(value, 64, 1)
    return value + pltpu.roll(value, 32, 1)


def primitives(state):
    inverse = 1.0 / state[0]
    vel = [state[k] * inverse for k in (1, 2, 3)]
    kinetic = 0.5 * state[0] * (vel[0] * vel[0] + vel[1] * vel[1] + vel[2] * vel[2])
    return [state[0], *vel, (GAMMA - 1.0) * (state[4] - kinetic)]


def exchange_kernel(
    sizes, fields_hbm, new_source_hbm, ghost_hbm, moved, packed, top,
    fields, new_source, ghost, load_sems, strips, move_out, move_in, face_out, face_in, top_out, top_in, top_out2, top_in2,
    move_sems, face_sems, top_sems, top_sems2,
):
    curves, subs = sizes
    count = curves * subs
    slots = fields.shape[0]
    loads = [
        pltpu.make_async_copy(new_source_hbm, new_source, load_sems.at[0]),
        pltpu.make_async_copy(fields_hbm, fields, load_sems.at[1]),
        pltpu.make_async_copy(ghost_hbm, ghost, load_sems.at[2]),
    ]
    for copy in loads:
        copy.start()
    curve, sub = lax.axis_index("curve"), lax.axis_index("sub")
    here = curve * subs + sub

    def at(shift):
        other = lax.rem(here + shift + count, count)
        return (other // subs, lax.rem(other, subs))

    sub_peers = [(curve, lax.rem(sub + k, subs)) for k in range(1, subs)]
    curve_peers = [(lax.rem(curve + k, curves), sub) for k in range(1, curves)]
    barrier = pltpu.get_barrier_semaphore()
    peers = sub_peers + curve_peers + [at(s) for s in SHIFTS]
    for peer in peers:
        pl.semaphore_signal(barrier, inc=1, device_id=peer, device_id_type=MESH)

    loads[0].wait()
    loads[1].wait()
    base = here * slots
    for n, shift in enumerate((1, -1)):
        receiver = lax.rem(here + shift + count, count)
        pick = jnp.int32(0)
        for j in range(slots):
            source = new_source[receiver * slots + j] - base
            pick = jnp.where((source >= 0) & (source < slots), source, pick)
        move_out[n] = fields[pick]

    around = [
        new_source[lax.rem(here + s + count, count) * slots + j]
        for s in (-1, 0, 1)
        for j in range(slots)
    ]
    fastest = jnp.zeros((8, 128), jnp.float32)
    for b in range(slots):
        used = jnp.int32(0)
        for source in around:
            used = jnp.where(source == base + b, 1, used)
        prim = primitives([fields[b, k] for k in range(5)])
        quick = jnp.maximum(jnp.maximum(jnp.abs(prim[1]), jnp.abs(prim[2])), jnp.abs(prim[3]))
        quick = quick + jnp.sqrt(GAMMA * prim[4] / prim[0])
        quick = jnp.where(used > 0, quick, 0.0)
        for r in (0, 8):
            for c in (0, 128):
                fastest = jnp.maximum(fastest, quick[r : r + 8, c : c + 128])
    top_out[...] = fastest

    pl.semaphore_wait(barrier, len(peers))

    firsts = []
    for n, peer in enumerate(sub_peers):
        firsts.append(
            pltpu.make_async_remote_copy(
                top_out, top_in.at[n], top_sems.at[0, n], top_sems.at[1, n],
                device_id=peer, device_id_type=MESH,
            )
        )
        firsts[-1].start()
    moves = []
    for k in range(5):
        for n, shift in enumerate((1, -1)):
            moves.append(
                pltpu.make_async_remote_copy(
                    move_out.at[n, k], move_in.at[n, k],
                    move_sems.at[0, n, k], move_sems.at[1, n, k],
                    device_id=at(shift), device_id_type=MESH,
                )
            )
            moves[-1].start()

    loads[2].wait()
    picks = []
    for shift in (0,) + SHIFTS:
        receiver = lax.rem(here + shift + count, count)
        rank = jnp.int32(0)
        chosen = [jnp.int32(0)] * CAPG
        for j in range(slots):
            for f in range(6):
                source = ghost[f, receiver * slots + j] - base
                going = (source >= 0) & (source < slots)
                row = source * 6 + SIDES[f]
                for k in range(CAPG):
                    chosen[k] = jnp.where(going & (rank == k), row, chosen[k])
                rank = rank + jnp.where(going, 1, 0)
        picks.append(chosen)

    own = [new_source[base + j] for j in range(slots)]
    cell, column = iota((256, 256), 0), iota((256, 256), 1)
    inside = lax.rem(column, 32)
    wanted_cell = (inside // 2) * 16 + lax.rem(inside, 2) + jnp.where(column >= 128, 14, 0)
    x_picker = jnp.where(cell == wanted_cell, 1.0, 0.0).astype(jnp.bfloat16)
    lane16 = iota((16, 128), 1)
    lane8, row8 = iota((8, 128), 1), iota((8, 128), 0)
    group_here = (lane8 // 32) == lax.rem(row8, 4)

    group = iota((16, 128), 1) // 32

    def gathered(chosen, k):
        value = strips[chosen[0], k]
        for i in range(1, CAPG):
            value = jnp.where(group == i, strips[chosen[i], k], value)
        return value

    def second_stage():
        for copy in firsts:
            copy.wait()
        fastest = top_out[...]
        for n in range(subs - 1):
            fastest = jnp.maximum(fastest, top_in[n])
        top_out2[...] = fastest
        copies = []
        for n, peer in enumerate(curve_peers):
            copies.append(
                pltpu.make_async_remote_copy(
                    top_out2, top_in2.at[n], top_sems2.at[0, n], top_sems2.at[1, n],
                    device_id=peer, device_id_type=MESH,
                )
            )
            copies[-1].start()
        return copies

    faces = []
    for k in range(5):
        moves[2 * k].wait()
        moves[2 * k + 1].wait()
        boxes = []
        for j in range(slots):
            source = own[j] - base
            local = (source >= 0) & (source < slots)
            slot = jnp.where(local, source, 0)
            value = jnp.where(source < 0, move_in[0, k], move_in[1, k])
            value = jnp.where(local, fields[slot, k], value)
            boxes.append(jnp.where(own[j] >= 0, value, FILLER[k]))
            moved[j, k] = boxes[j]
        x_strips = picked(jnp.concatenate(boxes, axis=0), x_picker)
        for j, box in enumerate(boxes):
            strips[j * 6 + 0, k] = x_strips[j * 16 : j * 16 + 16, :128]
            strips[j * 6 + 1, k] = x_strips[j * 16 : j * 16 + 16, 128:]
            strips[j * 6 + 2, k] = repeated(jnp.where(lane16 < 32, box[:, :128], 0.0))
            strips[j * 6 + 3, k] = repeated(jnp.where(lane16 >= 96, box[:, 128:], 0.0))
            for side, first in ((4, 0), (5, 14)):
                for layer in range(2):
                    line = box[first + layer : first + layer + 1]
                    spread = jnp.where(
                        row8 < 4,
                        jnp.broadcast_to(line[:, :128], (8, 128)),
                        jnp.broadcast_to(line[:, 128:], (8, 128)),
                    )
                    strips[j * 6 + side, k, pl.ds(layer * 8, 8)] = repeated(
                        jnp.where(group_here, spread, 0.0)
                    )
        for n, shift in enumerate(SHIFTS):
            face_out[n, k] = gathered(picks[n + 1], k)
            faces.append(
                pltpu.make_async_remote_copy(
                    face_out.at[n, k], face_in.at[n, k],
                    face_sems.at[0, n, k], face_sems.at[1, n, k],
                    device_id=at(shift), device_id_type=MESH,
                )
            )
            faces[-1].start()
        packed[0, k] = gathered(picks[0], k)
        if k == 0:
            seconds = second_stage()
    for copy in seconds:
        copy.wait()
    fastest = top_out2[...]
    for n in range(curves - 1):
        fastest = jnp.maximum(fastest, top_in2[n])
    top[...] = fastest
    for k in range(5):
        for n in range(len(SHIFTS)):
            faces[k * len(SHIFTS) + n].wait()
            packed[n + 1, k] = face_in[n, k]


def earlier(pair, axis):
    box, ghost = pair
    if axis == 0:
        edge = iota((16, 256), 1) % 16 == 0
        return (
            jnp.where(edge, pltpu.roll(ghost, 241, 1), pltpu.roll(box, 1, 1)),
            jnp.where(edge, pltpu.roll(box, 241, 1), pltpu.roll(ghost, 1, 1)),
        )
    if axis == 1:
        box, ghost = pltpu.roll(box, 16, 1), pltpu.roll(ghost, 16, 1)
        edge = iota((16, 128), 1) < 16
        low = box[:, :128]
        return (
            jnp.concatenate([jnp.where(edge, ghost, low), box[:, 128:]], axis=1),
            jnp.where(edge, low, ghost),
        )
    box, ghost = pltpu.roll(box, 1, 0), pltpu.roll(ghost, 1, 0)
    edge = iota((8, 256), 0) == 0
    low = box[:8]
    return (
        jnp.concatenate([jnp.where(edge, ghost, low), box[8:]], axis=0),
        jnp.where(edge, low, ghost),
    )


def later(pair, axis):
    box, ghost = pair
    if axis == 0:
        edge = iota((16, 256), 1) % 16 == 15
        return (
            jnp.where(edge, pltpu.roll(ghost, 15, 1), pltpu.roll(box, 255, 1)),
            jnp.where(edge, pltpu.roll(box, 15, 1), pltpu.roll(ghost, 255, 1)),
        )
    if axis == 1:
        box, ghost = pltpu.roll(box, 240, 1), pltpu.roll(ghost, 112, 1)
        edge = iota((16, 128), 1) >= 112
        high = box[:, 128:]
        return (
            jnp.concatenate([box[:, :128], jnp.where(edge, ghost, high)], axis=1),
            jnp.where(edge, high, ghost),
        )
    box, ghost = pltpu.roll(box, 15, 0), pltpu.roll(ghost, 7, 0)
    edge = iota((8, 256), 0) == 7
    high = box[8:]
    return (
        jnp.concatenate([box[:8], jnp.where(edge, ghost, high)], axis=0),
        jnp.where(edge, high, ghost),
    )


def euler_terms(prim, axis):
    density, vel, pressure = prim[0], prim[1:4], prim[4]
    along = vel[axis]
    energy = pressure * (1.0 / (GAMMA - 1.0)) + 0.5 * density * (
        vel[0] * vel[0] + vel[1] * vel[1] + vel[2] * vel[2]
    )
    conserved = [density, density * vel[0], density * vel[1], density * vel[2], energy]
    fluxes = [value * along for value in conserved]
    fluxes[axis + 1] = fluxes[axis + 1] + pressure
    fluxes[4] = fluxes[4] + pressure * along
    return conserved, fluxes, jnp.abs(along) + jnp.sqrt(GAMMA * pressure / density)


def face_flux(left, right, axis):
    cons_l, flux_l, speed_l = euler_terms(left, axis)
    cons_r, flux_r, speed_r = euler_terms(right, axis)
    speed = jnp.maximum(speed_l, speed_r)
    return [0.5 * (flux_l[k] + flux_r[k]) - 0.5 * speed * (cons_r[k] - cons_l[k]) for k in range(5)]


def sweep(prim, prim_ghost, axis):
    lefts, rights = ([], []), ([], [])
    for k in range(5):
        pair = (prim[k], prim_ghost[k])
        before = earlier(pair, axis)
        step = (pair[0] - before[0], pair[1] - before[1])
        after = later(step, axis)
        ends = []
        for i in range(2):
            slope = jnp.maximum(0.0, jnp.minimum(step[i], after[i])) + jnp.minimum(
                0.0, jnp.maximum(step[i], after[i])
            )
            ends.append(pair[i] + 0.5 * slope)
            rights[i].append(pair[i] - 0.5 * slope)
        before = earlier(ends, axis)
        lefts[0].append(before[0])
        lefts[1].append(before[1])
    inner = face_flux(lefts[0], rights[0], axis)
    outer = face_flux(lefts[1], rights[1], axis)
    return [later((inner[k], outer[k]), axis)[0] - inner[k] for k in range(5)]


def advance_kernel(sizes, moved, packed, top, new_source, ghost, out, where_from):
    curves, subs = sizes
    count = curves * subs
    slots = moved.shape[0]
    here = lax.axis_index("curve") * subs + lax.axis_index("sub")
    base = here * slots
    ranks = [jnp.int32(0)] * 5
    for j in range(slots):
        for f in range(6):
            source = ghost[f, base + j]
            row, group = jnp.int32(0), jnp.int32(-1)
            for n, shift in enumerate((0,) + SHIFTS):
                offset = source - lax.rem(here - shift + count, count) * slots
                hit = (offset >= 0) & (offset < slots)
                row = jnp.where(hit, n, row)
                group = jnp.where(hit, ranks[n], group)
                ranks[n] = ranks[n] + jnp.where(hit, 1, 0)
            where_from[0, j * 6 + f] = row
            where_from[1, j * 6 + f] = group
    ratio = COURANT / jnp.max(top[...])
    row_in, column = iota((256, 256), 0), iota((256, 256), 1)
    x = column % 16
    low_cell = (column // 16) * 2 + x - 14
    high_cell = 128 + (column // 16) * 2 + x
    x_spread = jnp.where(
        ((x >= 14) & (row_in == low_cell)) | ((x < 2) & (row_in == high_cell)), 1.0, 0.0
    ).astype(jnp.bfloat16)
    lane, row16 = iota((16, 128), 1), iota((16, 128), 0)
    row_wide = iota((8, 256), 0)

    @pl.loop(0, slots)
    def _(j):
        def strip(f, k):
            group = where_from[1, j * 6 + f]
            value = packed[where_from[0, j * 6 + f], k]
            value = repeated(jnp.where(lane // 32 == group, value, 0.0))
            return jnp.where(group >= 0, value, FILLER[k])

        def z_lines(f, k):
            value = jnp.where(lane // 32 == row16 % 4, strip(f, k), 0.0)
            sums = [jnp.sum(value[4 * i : 4 * i + 4], axis=0, keepdims=True) for i in range(4)]
            return [jnp.concatenate(sums[2 * i : 2 * i + 2], axis=1) for i in range(2)]

        box = [moved[j, k] for k in range(5)]
        prim = primitives(box)
        total = None
        for axis in range(3):
            ghosts, sides = [], []
            for k in range(5):
                if axis < 2:
                    low, high = strip(2 * axis, k), strip(2 * axis + 1, k)
                if axis == 0:
                    sides.append(jnp.concatenate([low, high], axis=1))
                elif axis == 1:
                    ghosts.append(jnp.where(lane < 64, high, low))
                else:
                    low, high = z_lines(4, k), z_lines(5, k)
                    value = jnp.where(row_wide == 6, low[0], low[1])
                    value = jnp.where(row_wide == 1, high[1], value)
                    ghosts.append(jnp.where(row_wide == 0, high[0], value))
            if axis == 0:
                spread = picked(jnp.concatenate(sides, axis=0), x_spread)
                ghosts = [spread[16 * k : 16 * k + 16] for k in range(5)]
            change = sweep(prim, primitives(ghosts), axis)
            total = change if total is None else [a + b for a, b in zip(total, change)]
        taken = new_source[base + j] >= 0
        for k in range(5):
            out[j, k] = jnp.where(taken, box[k] - ratio * total[k], 0.0)


def body(sizes, fields, new_source, ghost_source):
    curves, subs = sizes
    slots = fields.shape[0]
    ghost = ghost_source.T
    f32 = jnp.float32
    tile = (5, 16, 128)
    moved, packed, top = pl.pallas_call(
        functools.partial(exchange_kernel, sizes),
        out_shape=[
            jax.ShapeDtypeStruct(fields.shape, f32),
            jax.ShapeDtypeStruct((5,) + tile, f32),
            jax.ShapeDtypeStruct((8, 128), f32),
        ],
        in_specs=[pl.BlockSpec(memory_space=pltpu.HBM)] * 3,
        out_specs=[VMEM] * 3,
        scratch_shapes=[
            pltpu.VMEM(fields.shape, f32),
            pltpu.SMEM(new_source.shape, jnp.int32),
            pltpu.SMEM(ghost.shape, jnp.int32),
            pltpu.SemaphoreType.DMA((3,)),
            pltpu.VMEM((slots * 6,) + tile, f32),
            pltpu.VMEM((2,) + fields.shape[1:], f32),
            pltpu.VMEM((2,) + fields.shape[1:], f32),
            pltpu.VMEM((4,) + tile, f32),
            pltpu.VMEM((4,) + tile, f32),
            pltpu.VMEM((8, 128), f32),
            pltpu.VMEM((subs - 1, 8, 128), f32),
            pltpu.VMEM((8, 128), f32),
            pltpu.VMEM((curves - 1, 8, 128), f32),
            pltpu.SemaphoreType.DMA((2, 2, 5)),
            pltpu.SemaphoreType.DMA((2, 4, 5)),
            pltpu.SemaphoreType.DMA((2, subs - 1)),
            pltpu.SemaphoreType.DMA((2, curves - 1)),
        ],
        compiler_params=pltpu.CompilerParams(
            collective_id=0, has_side_effects=True, vmem_limit_bytes=24 << 20
        ),
    )(fields, new_source, ghost)
    return pl.pallas_call(
        functools.partial(advance_kernel, sizes),
        out_shape=jax.ShapeDtypeStruct(fields.shape, f32),
        in_specs=[VMEM, VMEM, VMEM, SMEM, SMEM],
        out_specs=VMEM,
        scratch_shapes=[pltpu.SMEM((2, slots * 6), jnp.int32)],
        compiler_params=pltpu.CompilerParams(vmem_limit_bytes=24 << 20),
    )(moved, packed, top, new_source, ghost)


def solution(mesh):
    placed = P(("curve", "sub"), None, None, None)
    sizes = (mesh.shape["curve"], mesh.shape["sub"])
    return jax.shard_map(
        functools.partial(body, sizes),
        mesh=mesh,
        in_specs=(placed, P(), P()),
        out_specs=placed,
        check_vma=False,
    )
```

```python
import functools

import jax
import jax.numpy as jnp
from jax import lax
from jax.experimental import pallas as pl
from jax.experimental.pallas import tpu as pltpu
from jax.sharding import PartitionSpec as P

MESH = pl.DeviceIdType.MESH
SHIFTS = (1, -1, 2, -2)
CAPG = 4
SIDES = (1, 0, 3, 2, 5, 4)
GAMMA = 5.0 / 3.0
COURANT = 0.3
FILLER = (1.0, 0.0, 0.0, 0.0, 1.5)
VMEM = pl.BlockSpec(memory_space=pltpu.VMEM)


def iota(shape, dim):
    return lax.broadcasted_iota(jnp.int32, shape, dim)


def picked(values, one_hot):
    rows = values.shape[0]
    parts = []
    for _ in range(3):
        parts.append(values.astype(jnp.bfloat16))
        values = values - parts[-1].astype(jnp.float32)
    product = jnp.dot(jnp.concatenate(parts, axis=0), one_hot, preferred_element_type=jnp.float32)
    return product[:rows] + product[rows : 2 * rows] + product[2 * rows :]


def repeated(value):
    value = value + pltpu.roll(value, 64, 1)
    return value + pltpu.roll(value, 32, 1)


def primitives(state):
    inverse = 1.0 / state[0]
    vel = [state[k] * inverse for k in (1, 2, 3)]
    kinetic = 0.5 * state[0] * (vel[0] * vel[0] + vel[1] * vel[1] + vel[2] * vel[2])
    return [state[0], *vel, (GAMMA - 1.0) * (state[4] - kinetic)]


def before(value, axis):
    return pltpu.roll(value, (1, 16, 1)[axis], (1, 1, 0)[axis])


def after(value, axis):
    return pltpu.roll(value, (255, 240, 15)[axis], (1, 1, 0)[axis])


def euler_terms(prim, axis):
    density, vel, pressure = prim[0], prim[1:4], prim[4]
    along = vel[axis]
    energy = pressure * (1.0 / (GAMMA - 1.0)) + 0.5 * density * (
        vel[0] * vel[0] + vel[1] * vel[1] + vel[2] * vel[2]
    )
    conserved = [density, density * vel[0], density * vel[1], density * vel[2], energy]
    fluxes = [value * along for value in conserved]
    fluxes[axis + 1] = fluxes[axis + 1] + pressure
    fluxes[4] = fluxes[4] + pressure * along
    return conserved, fluxes, jnp.abs(along) + jnp.sqrt(GAMMA * pressure / density)


def face_flux(left, right, axis):
    cons_l, flux_l, speed_l = euler_terms(left, axis)
    cons_r, flux_r, speed_r = euler_terms(right, axis)
    speed = jnp.maximum(speed_l, speed_r)
    return [0.5 * (flux_l[k] + flux_r[k]) - 0.5 * speed * (cons_r[k] - cons_l[k]) for k in range(5)]


def sweep(prim, axis):
    lefts, rights = [], []
    for value in prim:
        step = value - before(value, axis)
        ahead = after(step, axis)
        slope = jnp.maximum(0.0, jnp.minimum(step, ahead)) + jnp.minimum(
            0.0, jnp.maximum(step, ahead)
        )
        rights.append(value - 0.5 * slope)
        lefts.append(before(value + 0.5 * slope, axis))
    flux = face_flux(lefts, rights, axis)
    return [after(value, axis) - value for value in flux]


def step_kernel(
    sizes, fields_hbm, new_source_hbm, ghost_hbm, out, moved, packed, partial, where_from,
    fields, new_source, ghost, load_sems, strips, move_out, move_in, face_out, face_in, top_out, top_in, top_out2, top_in2,
    move_sems, face_sems, top_sems, top_sems2,
):
    curves, subs = sizes
    count = curves * subs
    slots = fields.shape[0]
    loads = [
        pltpu.make_async_copy(new_source_hbm, new_source, load_sems.at[0]),
        pltpu.make_async_copy(fields_hbm, fields, load_sems.at[1]),
        pltpu.make_async_copy(ghost_hbm, ghost, load_sems.at[2]),
    ]
    for copy in loads:
        copy.start()
    curve, sub = lax.axis_index("curve"), lax.axis_index("sub")
    here = curve * subs + sub

    def at(shift):
        other = lax.rem(here + shift + count, count)
        return (other // subs, lax.rem(other, subs))

    sub_peers = [(curve, lax.rem(sub + k, subs)) for k in range(1, subs)]
    curve_peers = [(lax.rem(curve + k, curves), sub) for k in range(1, curves)]
    barrier = pltpu.get_barrier_semaphore()
    peers = sub_peers + curve_peers + [at(s) for s in SHIFTS]
    for peer in peers:
        pl.semaphore_signal(barrier, inc=1, device_id=peer, device_id_type=MESH)

    loads[0].wait()
    loads[1].wait()
    base = here * slots
    for n, shift in enumerate((1, -1)):
        receiver = lax.rem(here + shift + count, count)
        pick = jnp.int32(0)
        for j in range(slots):
            source = new_source[receiver * slots + j] - base
            pick = jnp.where((source >= 0) & (source < slots), source, pick)
        move_out[n] = fields[pick]

    around = [
        new_source[lax.rem(here + s + count, count) * slots + j]
        for s in (-1, 0, 1)
        for j in range(slots)
    ]
    fastest = jnp.zeros((8, 128), jnp.float32)
    for b in range(slots):
        used = jnp.int32(0)
        for source in around:
            used = jnp.where(source == base + b, 1, used)
        prim = primitives([fields[b, k] for k in range(5)])
        quick = jnp.maximum(jnp.maximum(jnp.abs(prim[1]), jnp.abs(prim[2])), jnp.abs(prim[3]))
        quick = quick + jnp.sqrt(GAMMA * prim[4] / prim[0])
        quick = jnp.where(used > 0, quick, 0.0)
        for r in (0, 8):
            for c in (0, 128):
                fastest = jnp.maximum(fastest, quick[r : r + 8, c : c + 128])
    top_out[...] = fastest

    pl.semaphore_wait(barrier, len(peers))

    firsts = []
    for n, peer in enumerate(sub_peers):
        firsts.append(
            pltpu.make_async_remote_copy(
                top_out, top_in.at[n], top_sems.at[0, n], top_sems.at[1, n],
                device_id=peer, device_id_type=MESH,
            )
        )
        firsts[-1].start()
    moves = []
    for k in range(5):
        for n, shift in enumerate((1, -1)):
            moves.append(
                pltpu.make_async_remote_copy(
                    move_out.at[n, k], move_in.at[n, k],
                    move_sems.at[0, n, k], move_sems.at[1, n, k],
                    device_id=at(shift), device_id_type=MESH,
                )
            )
            moves[-1].start()

    loads[2].wait()
    picks = []
    for shift in (0,) + SHIFTS:
        receiver = lax.rem(here + shift + count, count)
        rank = jnp.int32(0)
        chosen = [jnp.int32(0)] * CAPG
        for j in range(slots):
            for f in range(6):
                source = ghost[f, receiver * slots + j] - base
                going = (source >= 0) & (source < slots)
                row = source * 6 + SIDES[f]
                for k in range(CAPG):
                    chosen[k] = jnp.where(going & (rank == k), row, chosen[k])
                rank = rank + jnp.where(going, 1, 0)
        picks.append(chosen)

    ranks = [jnp.int32(0)] * 5
    for j in range(slots):
        for f in range(6):
            source = ghost[f, base + j]
            row, place = jnp.int32(0), jnp.int32(-1)
            for n, shift in enumerate((0,) + SHIFTS):
                offset = source - lax.rem(here - shift + count, count) * slots
                hit = (offset >= 0) & (offset < slots)
                row = jnp.where(hit, n, row)
                place = jnp.where(hit, ranks[n], place)
                ranks[n] = ranks[n] + jnp.where(hit, 1, 0)
            where_from[0, j * 6 + f] = row
            where_from[1, j * 6 + f] = place
    own = [new_source[base + j] for j in range(slots)]
    cell, column = iota((256, 256), 0), iota((256, 256), 1)
    inside = lax.rem(column, 32)
    wanted_cell = (inside // 2) * 16 + lax.rem(inside, 2) + jnp.where(column >= 128, 14, 0)
    x_picker = jnp.where(cell == wanted_cell, 1.0, 0.0).astype(jnp.bfloat16)
    lane16 = iota((16, 128), 1)
    lane8, row8 = iota((8, 128), 1), iota((8, 128), 0)
    group_here = (lane8 // 32) == lax.rem(row8, 4)

    group = iota((16, 128), 1) // 32

    def gathered(chosen, k):
        value = strips[chosen[0], k]
        for i in range(1, CAPG):
            value = jnp.where(group == i, strips[chosen[i], k], value)
        return value

    def second_stage():
        for copy in firsts:
            copy.wait()
        fastest = top_out[...]
        for n in range(subs - 1):
            fastest = jnp.maximum(fastest, top_in[n])
        top_out2[...] = fastest
        copies = []
        for n, peer in enumerate(curve_peers):
            copies.append(
                pltpu.make_async_remote_copy(
                    top_out2, top_in2.at[n], top_sems2.at[0, n], top_sems2.at[1, n],
                    device_id=peer, device_id_type=MESH,
                )
            )
            copies[-1].start()
        return copies

    faces = []
    for k in range(5):
        moves[2 * k].wait()
        moves[2 * k + 1].wait()
        boxes = []
        for j in range(slots):
            source = own[j] - base
            local = (source >= 0) & (source < slots)
            slot = jnp.where(local, source, 0)
            value = jnp.where(source < 0, move_in[0, k], move_in[1, k])
            value = jnp.where(local, fields[slot, k], value)
            boxes.append(jnp.where(own[j] >= 0, value, FILLER[k]))
            moved[j, k] = boxes[j]
        x_strips = picked(jnp.concatenate(boxes, axis=0), x_picker)
        for j, box in enumerate(boxes):
            strips[j * 6 + 0, k] = x_strips[j * 16 : j * 16 + 16, :128]
            strips[j * 6 + 1, k] = x_strips[j * 16 : j * 16 + 16, 128:]
            strips[j * 6 + 2, k] = repeated(jnp.where(lane16 < 32, box[:, :128], 0.0))
            strips[j * 6 + 3, k] = repeated(jnp.where(lane16 >= 96, box[:, 128:], 0.0))
            for side, first in ((4, 0), (5, 14)):
                for layer in range(2):
                    line = box[first + layer : first + layer + 1]
                    spread = jnp.where(
                        row8 < 4,
                        jnp.broadcast_to(line[:, :128], (8, 128)),
                        jnp.broadcast_to(line[:, 128:], (8, 128)),
                    )
                    strips[j * 6 + side, k, pl.ds(layer * 8, 8)] = repeated(
                        jnp.where(group_here, spread, 0.0)
                    )
        for n, shift in enumerate(SHIFTS):
            face_out[n, k] = gathered(picks[n + 1], k)
            faces.append(
                pltpu.make_async_remote_copy(
                    face_out.at[n, k], face_in.at[n, k],
                    face_sems.at[0, n, k], face_sems.at[1, n, k],
                    device_id=at(shift), device_id_type=MESH,
                )
            )
            faces[-1].start()
        packed[0, k] = gathered(picks[0], k)
        if k == 0:
            seconds = second_stage()
    for copy in seconds:
        copy.wait()
    fastest = top_out2[...]
    for n in range(curves - 1):
        fastest = jnp.maximum(fastest, top_in2[n])
    ratio = COURANT / jnp.max(fastest)

    wide_lane, wide_row = iota((16, 256), 1), iota((16, 256), 0)
    places = (lax.rem(wide_lane, 16), wide_lane // 16, wide_row)

    @pl.loop(0, slots)
    def _(j):
        prim = primitives([moved[j, k] for k in range(5)])
        total = [0.0] * 5
        for axis in range(3):
            inner = (places[axis] >= 2) & (places[axis] < 14)
            change = sweep(prim, axis)
            total = [total[k] + jnp.where(inner, change[k], 0.0) for k in range(5)]
        for k in range(5):
            partial[j, k] = total[k]

    row_in, column = iota((256, 256), 0), iota((256, 256), 1)
    x = lax.rem(column, 16)
    low_cell = (column // 16) * 2 + x
    high_cell = 128 + (column // 16) * 2 + x - 14
    x_spread = jnp.where(
        ((x < 2) & (row_in == low_cell)) | ((x >= 14) & (row_in == high_cell)), 1.0, 0.0
    ).astype(jnp.bfloat16)
    row16 = iota((16, 128), 0)
    z_here = (lane16 // 32) == lax.rem(row16, 4)
    row_low = iota((8, 256), 0)

    for k in range(5):
        for n in range(len(SHIFTS)):
            faces[k * len(SHIFTS) + n].wait()
            packed[n + 1, k] = face_in[n, k]

    @pl.loop(0, slots)
    def _(j):
        def strip(f, k):
            group_of = where_from[1, j * 6 + f]
            value = packed[where_from[0, j * 6 + f], k]
            value = repeated(jnp.where(group == group_of, value, 0.0))
            return jnp.where(group_of >= 0, value, FILLER[k])

        def z_lines(f, k):
            value = jnp.where(z_here, strip(f, k), 0.0)
            sums = [jnp.sum(value[4 * i : 4 * i + 4], axis=0, keepdims=True) for i in range(4)]
            return [jnp.concatenate(sums[2 * i : 2 * i + 2], axis=1) for i in range(2)]

        box = [moved[j, k] for k in range(5)]
        prim = primitives(box)
        total = [partial[j, k] for k in range(5)]
        for axis in range(3):
            ghosts, sides = [], []
            for k in range(5):
                if axis == 0:
                    sides.append(jnp.concatenate([strip(0, k), strip(1, k)], axis=1))
                elif axis == 1:
                    ghosts.append(jnp.where(lane16 < 64, strip(2, k), strip(3, k)))
                else:
                    low, high = z_lines(4, k), z_lines(5, k)
                    value = jnp.where(row_low == 6, high[0], high[1])
                    value = jnp.where(row_low == 1, low[1], value)
                    ghosts.append(jnp.where(row_low == 0, low[0], value))
            if axis == 0:
                spread = picked(jnp.concatenate(sides, axis=0), x_spread)
                ghosts = [spread[16 * k : 16 * k + 16] for k in range(5)]
            rim = []
            for inside, ghost_value in zip(prim, primitives(ghosts)):
                if axis == 0:
                    value = jnp.where(
                        places[0] < 8, pltpu.roll(inside, 2, 1), pltpu.roll(inside, 254, 1)
                    )
                    ends = (places[0] < 2) | (places[0] >= 14)
                    rim.append(jnp.where(ends, ghost_value, value))
                elif axis == 1:
                    low = pltpu.roll(inside, 32, 1)[:, :128]
                    high = pltpu.roll(inside, 224, 1)[:, 128:]
                    low = jnp.where(lane16 < 32, ghost_value, low)
                    high = jnp.where(lane16 >= 96, ghost_value, high)
                    rim.append(jnp.concatenate([low, high], axis=1))
                else:
                    low = jnp.where(row_low < 2, ghost_value, pltpu.roll(inside, 2, 0)[:8])
                    high = jnp.where(row_low >= 6, ghost_value, pltpu.roll(inside, 14, 0)[8:])
                    rim.append(jnp.concatenate([low, high], axis=0))
            change = sweep(rim, axis)
            up, down, dim = ((2, 254, 1), (32, 224, 1), (2, 14, 0))[axis]
            for k in range(5):
                edge = jnp.where(places[axis] >= 14, pltpu.roll(change[k], up, dim), 0.0)
                edge = jnp.where(places[axis] < 2, pltpu.roll(change[k], down, dim), edge)
                total[k] = total[k] + edge
        taken = new_source[base + j] >= 0
        for k in range(5):
            out[j, k] = jnp.where(taken, box[k] - ratio * total[k], 0.0)


def body(sizes, fields, new_source, ghost_source):
    curves, subs = sizes
    slots = fields.shape[0]
    ghost = ghost_source.T
    f32 = jnp.float32
    tile = (5, 16, 128)
    return pl.pallas_call(
        functools.partial(step_kernel, sizes),
        out_shape=jax.ShapeDtypeStruct(fields.shape, f32),
        in_specs=[pl.BlockSpec(memory_space=pltpu.HBM)] * 3,
        out_specs=VMEM,
        scratch_shapes=[
            pltpu.VMEM(fields.shape, f32),
            pltpu.VMEM((5,) + tile, f32),
            pltpu.VMEM(fields.shape, f32),
            pltpu.SMEM((2, slots * 6), jnp.int32),
            pltpu.VMEM(fields.shape, f32),
            pltpu.SMEM(new_source.shape, jnp.int32),
            pltpu.SMEM(ghost.shape, jnp.int32),
            pltpu.SemaphoreType.DMA((3,)),
            pltpu.VMEM((slots * 6,) + tile, f32),
            pltpu.VMEM((2,) + fields.shape[1:], f32),
            pltpu.VMEM((2,) + fields.shape[1:], f32),
            pltpu.VMEM((4,) + tile, f32),
            pltpu.VMEM((4,) + tile, f32),
            pltpu.VMEM((8, 128), f32),
            pltpu.VMEM((subs - 1, 8, 128), f32),
            pltpu.VMEM((8, 128), f32),
            pltpu.VMEM((curves - 1, 8, 128), f32),
            pltpu.SemaphoreType.DMA((2, 2, 5)),
            pltpu.SemaphoreType.DMA((2, 4, 5)),
            pltpu.SemaphoreType.DMA((2, subs - 1)),
            pltpu.SemaphoreType.DMA((2, curves - 1)),
        ],
        compiler_params=pltpu.CompilerParams(
            collective_id=0, has_side_effects=True, vmem_limit_bytes=60 << 20
        ),
    )(fields, new_source, ghost)


def solution(mesh):
    placed = P(("curve", "sub"), None, None, None)
    sizes = (mesh.shape["curve"], mesh.shape["sub"])
    return jax.shard_map(
        functools.partial(body, sizes),
        mesh=mesh,
        in_specs=(placed, P(), P()),
        out_specs=placed,
        check_vma=False,
    )
```

```python
import functools

import jax
import jax.numpy as jnp
from jax import lax
from jax.experimental import pallas as pl
from jax.experimental.pallas import tpu as pltpu
from jax.sharding import PartitionSpec as P

MESH = pl.DeviceIdType.MESH
SHIFTS = (1, -1, 2, -2)
CAPG = 4
SIDES = (1, 0, 3, 2, 5, 4)
GAMMA = 5.0 / 3.0
COURANT = 0.3
FILLER = (1.0, 0.0, 0.0, 0.0, 1.5)


def iota(shape, dim):
    return lax.broadcasted_iota(jnp.int32, shape, dim)


def picked(values, one_hot):
    rows = values.shape[0]
    parts = []
    for _ in range(3):
        parts.append(values.astype(jnp.bfloat16))
        values = values - parts[-1].astype(jnp.float32)
    product = jnp.dot(jnp.concatenate(parts, axis=0), one_hot, preferred_element_type=jnp.float32)
    return product[:rows] + product[rows : 2 * rows] + product[2 * rows :]


def repeated(value):
    value = value + pltpu.roll(value, 64, 1)
    return value + pltpu.roll(value, 32, 1)


def primitives(state):
    inverse = 1.0 / state[0]
    vel = [state[k] * inverse for k in (1, 2, 3)]
    kinetic = 0.5 * state[0] * (vel[0] * vel[0] + vel[1] * vel[1] + vel[2] * vel[2])
    return [state[0], *vel, (GAMMA - 1.0) * (state[4] - kinetic)]


def before(value, axis):
    return pltpu.roll(value, (1, 16, 1)[axis], (1, 1, 0)[axis])


def after(value, axis):
    return pltpu.roll(value, (255, 240, 15)[axis], (1, 1, 0)[axis])


def euler_terms(prim, axis):
    density, vel, pressure = prim[0], prim[1:4], prim[4]
    along = vel[axis]
    energy = pressure * (1.0 / (GAMMA - 1.0)) + 0.5 * density * (
        vel[0] * vel[0] + vel[1] * vel[1] + vel[2] * vel[2]
    )
    conserved = [density, density * vel[0], density * vel[1], density * vel[2], energy]
    fluxes = [value * along for value in conserved]
    fluxes[axis + 1] = fluxes[axis + 1] + pressure
    fluxes[4] = fluxes[4] + pressure * along
    return conserved, fluxes, jnp.abs(along) + jnp.sqrt(GAMMA * pressure / density)


def face_flux(left, right, axis):
    cons_l, flux_l, speed_l = euler_terms(left, axis)
    cons_r, flux_r, speed_r = euler_terms(right, axis)
    speed = jnp.maximum(speed_l, speed_r)
    return [0.5 * (flux_l[k] + flux_r[k]) - 0.5 * speed * (cons_r[k] - cons_l[k]) for k in range(5)]


def sweep(prim, axis):
    lefts, rights = [], []
    for value in prim:
        step = value - before(value, axis)
        ahead = after(step, axis)
        slope = jnp.maximum(0.0, jnp.minimum(step, ahead)) + jnp.minimum(
            0.0, jnp.maximum(step, ahead)
        )
        rights.append(value - 0.5 * slope)
        lefts.append(before(value + 0.5 * slope, axis))
    flux = face_flux(lefts, rights, axis)
    return [after(value, axis) - value for value in flux]


def step_kernel(
    sizes, fields_hbm, new_source_hbm, ghost_hbm, out_hbm, out, out_sems, moved, packed, partial, where_from,
    fields, new_source, ghost, load_sems, strips, move_out, move_in, face_out, face_in, top_out, top_in, top_out2, top_in2,
    move_sems, face_sems, top_sems, top_sems2,
):
    curves, subs = sizes
    count = curves * subs
    slots = fields.shape[0]
    loads = [
        pltpu.make_async_copy(new_source_hbm, new_source, load_sems.at[0]),
        pltpu.make_async_copy(fields_hbm, fields, load_sems.at[1]),
        pltpu.make_async_copy(ghost_hbm, ghost, load_sems.at[2]),
    ]
    for copy in loads:
        copy.start()
    curve, sub = lax.axis_index("curve"), lax.axis_index("sub")
    here = curve * subs + sub

    def at(shift):
        other = lax.rem(here + shift + count, count)
        return (other // subs, lax.rem(other, subs))

    sub_peers = [(curve, lax.rem(sub + k, subs)) for k in range(1, subs)]
    curve_peers = [(lax.rem(curve + k, curves), sub) for k in range(1, curves)]
    barrier = pltpu.get_barrier_semaphore()
    peers = sub_peers + curve_peers + [at(s) for s in SHIFTS]
    for peer in peers:
        pl.semaphore_signal(barrier, inc=1, device_id=peer, device_id_type=MESH)

    loads[0].wait()
    loads[1].wait()
    base = here * slots
    for n, shift in enumerate((1, -1)):
        receiver = lax.rem(here + shift + count, count)
        pick = jnp.int32(0)
        for j in range(slots):
            source = new_source[receiver * slots + j] - base
            pick = jnp.where((source >= 0) & (source < slots), source, pick)
        move_out[n] = fields[pick]

    pl.semaphore_wait(barrier, len(peers))

    moves = []
    for k in range(5):
        for n, shift in enumerate((1, -1)):
            moves.append(
                pltpu.make_async_remote_copy(
                    move_out.at[n, k], move_in.at[n, k],
                    move_sems.at[0, n, k], move_sems.at[1, n, k],
                    device_id=at(shift), device_id_type=MESH,
                )
            )
            moves[-1].start()

    around = [
        new_source[lax.rem(here + s + count, count) * slots + j]
        for s in (-1, 0, 1)
        for j in range(slots)
    ]
    fastest = jnp.zeros((8, 128), jnp.float32)
    for b in range(slots):
        used = jnp.int32(0)
        for source in around:
            used = jnp.where(source == base + b, 1, used)
        prim = primitives([fields[b, k] for k in range(5)])
        quick = jnp.maximum(jnp.maximum(jnp.abs(prim[1]), jnp.abs(prim[2])), jnp.abs(prim[3]))
        quick = quick + jnp.sqrt(GAMMA * prim[4] / prim[0])
        quick = jnp.where(used > 0, quick, 0.0)
        for r in (0, 8):
            for c in (0, 128):
                fastest = jnp.maximum(fastest, quick[r : r + 8, c : c + 128])
    top_out[...] = fastest

    firsts = []
    for n, peer in enumerate(sub_peers):
        firsts.append(
            pltpu.make_async_remote_copy(
                top_out, top_in.at[n], top_sems.at[0, n], top_sems.at[1, n],
                device_id=peer, device_id_type=MESH,
            )
        )
        firsts[-1].start()
    loads[2].wait()
    picks = []
    for shift in (0,) + SHIFTS:
        receiver = lax.rem(here + shift + count, count)
        rank = jnp.int32(0)
        chosen = [jnp.int32(0)] * CAPG
        for j in range(slots):
            for f in range(6):
                source = ghost[f, receiver * slots + j] - base
                going = (source >= 0) & (source < slots)
                row = source * 6 + SIDES[f]
                for k in range(CAPG):
                    chosen[k] = jnp.where(going & (rank == k), row, chosen[k])
                rank = rank + jnp.where(going, 1, 0)
        picks.append(chosen)

    ranks = [jnp.int32(0)] * 5
    for j in range(slots):
        for f in range(6):
            source = ghost[f, base + j]
            row, place = jnp.int32(0), jnp.int32(-1)
            for n, shift in enumerate((0,) + SHIFTS):
                offset = source - lax.rem(here - shift + count, count) * slots
                hit = (offset >= 0) & (offset < slots)
                row = jnp.where(hit, n, row)
                place = jnp.where(hit, ranks[n], place)
                ranks[n] = ranks[n] + jnp.where(hit, 1, 0)
            where_from[0, j * 6 + f] = row
            where_from[1, j * 6 + f] = place
    own = [new_source[base + j] for j in range(slots)]
    cell, column = iota((256, 256), 0), iota((256, 256), 1)
    inside = lax.rem(column, 32)
    wanted_cell = (inside // 2) * 16 + lax.rem(inside, 2) + jnp.where(column >= 128, 14, 0)
    x_picker = jnp.where(cell == wanted_cell, 1.0, 0.0).astype(jnp.bfloat16)
    lane16 = iota((16, 128), 1)
    lane8, row8 = iota((8, 128), 1), iota((8, 128), 0)
    group_here = (lane8 // 32) == lax.rem(row8, 4)

    group = iota((16, 128), 1) // 32

    def gathered(chosen, k):
        value = strips[chosen[0], k]
        for i in range(1, CAPG):
            value = jnp.where(group == i, strips[chosen[i], k], value)
        return value

    def second_stage():
        for copy in firsts:
            copy.wait()
        fastest = top_out[...]
        for n in range(subs - 1):
            fastest = jnp.maximum(fastest, top_in[n])
        top_out2[...] = fastest
        copies = []
        for n, peer in enumerate(curve_peers):
            copies.append(
                pltpu.make_async_remote_copy(
                    top_out2, top_in2.at[n], top_sems2.at[0, n], top_sems2.at[1, n],
                    device_id=peer, device_id_type=MESH,
                )
            )
            copies[-1].start()
        return copies

    faces = []
    for k in range(5):
        moves[2 * k].wait()
        moves[2 * k + 1].wait()
        boxes = []
        for j in range(slots):
            source = own[j] - base
            local = (source >= 0) & (source < slots)
            slot = jnp.where(local, source, 0)
            value = jnp.where(source < 0, move_in[0, k], move_in[1, k])
            value = jnp.where(local, fields[slot, k], value)
            boxes.append(jnp.where(own[j] >= 0, value, FILLER[k]))
            moved[j, k] = boxes[j]
        x_strips = picked(jnp.concatenate(boxes, axis=0), x_picker)
        for j, box in enumerate(boxes):
            strips[j * 6 + 0, k] = x_strips[j * 16 : j * 16 + 16, :128]
            strips[j * 6 + 1, k] = x_strips[j * 16 : j * 16 + 16, 128:]
            strips[j * 6 + 2, k] = repeated(jnp.where(lane16 < 32, box[:, :128], 0.0))
            strips[j * 6 + 3, k] = repeated(jnp.where(lane16 >= 96, box[:, 128:], 0.0))
            for side, first in ((4, 0), (5, 14)):
                for layer in range(2):
                    line = box[first + layer : first + layer + 1]
                    spread = jnp.where(
                        row8 < 4,
                        jnp.broadcast_to(line[:, :128], (8, 128)),
                        jnp.broadcast_to(line[:, 128:], (8, 128)),
                    )
                    strips[j * 6 + side, k, pl.ds(layer * 8, 8)] = repeated(
                        jnp.where(group_here, spread, 0.0)
                    )
        for n, shift in enumerate(SHIFTS):
            face_out[n, k] = gathered(picks[n + 1], k)
            faces.append(
                pltpu.make_async_remote_copy(
                    face_out.at[n, k], face_in.at[n, k],
                    face_sems.at[0, n, k], face_sems.at[1, n, k],
                    device_id=at(shift), device_id_type=MESH,
                )
            )
            faces[-1].start()
        packed[0, k] = gathered(picks[0], k)
    seconds = second_stage()

    wide_lane, wide_row = iota((16, 256), 1), iota((16, 256), 0)
    places = (lax.rem(wide_lane, 16), wide_lane // 16, wide_row)

    @pl.loop(0, slots)
    def _(j):
        prim = primitives([moved[j, k] for k in range(5)])
        total = [0.0] * 5
        for axis in range(3):
            inner = (places[axis] >= 2) & (places[axis] < 14)
            change = sweep(prim, axis)
            total = [total[k] + jnp.where(inner, change[k], 0.0) for k in range(5)]
        for k in range(5):
            partial[j, k] = total[k]

    row_in, column = iota((256, 256), 0), iota((256, 256), 1)
    x = lax.rem(column, 16)
    low_cell = (column // 16) * 2 + x
    high_cell = 128 + (column // 16) * 2 + x - 14
    x_spread = jnp.where(
        ((x < 2) & (row_in == low_cell)) | ((x >= 14) & (row_in == high_cell)), 1.0, 0.0
    ).astype(jnp.bfloat16)
    row16 = iota((16, 128), 0)
    z_here = (lane16 // 32) == lax.rem(row16, 4)
    row_low = iota((8, 256), 0)

    for copy in seconds:
        copy.wait()
    fastest = top_out2[...]
    for n in range(curves - 1):
        fastest = jnp.maximum(fastest, top_in2[n])
    ratio = COURANT / jnp.max(fastest)
    for k in range(5):
        for n in range(len(SHIFTS)):
            faces[k * len(SHIFTS) + n].wait()
            packed[n + 1, k] = face_in[n, k]

    @pl.loop(0, slots)
    def _(j):
        def strip(f, k):
            group_of = where_from[1, j * 6 + f]
            value = packed[where_from[0, j * 6 + f], k]
            value = repeated(jnp.where(group == group_of, value, 0.0))
            return jnp.where(group_of >= 0, value, FILLER[k])

        def z_lines(f, k):
            value = jnp.where(z_here, strip(f, k), 0.0)
            sums = [jnp.sum(value[4 * i : 4 * i + 4], axis=0, keepdims=True) for i in range(4)]
            return [jnp.concatenate(sums[2 * i : 2 * i + 2], axis=1) for i in range(2)]

        box = [moved[j, k] for k in range(5)]
        prim = primitives(box)
        total = [partial[j, k] for k in range(5)]
        for axis in range(3):
            ghosts, sides = [], []
            for k in range(5):
                if axis == 0:
                    sides.append(jnp.concatenate([strip(0, k), strip(1, k)], axis=1))
                elif axis == 1:
                    ghosts.append(jnp.where(lane16 < 64, strip(2, k), strip(3, k)))
                else:
                    low, high = z_lines(4, k), z_lines(5, k)
                    value = jnp.where(row_low == 6, high[0], high[1])
                    value = jnp.where(row_low == 1, low[1], value)
                    ghosts.append(jnp.where(row_low == 0, low[0], value))
            if axis == 0:
                spread = picked(jnp.concatenate(sides, axis=0), x_spread)
                ghosts = [spread[16 * k : 16 * k + 16] for k in range(5)]
            rim = []
            for inside, ghost_value in zip(prim, primitives(ghosts)):
                if axis == 0:
                    value = jnp.where(
                        places[0] < 8, pltpu.roll(inside, 2, 1), pltpu.roll(inside, 254, 1)
                    )
                    ends = (places[0] < 2) | (places[0] >= 14)
                    rim.append(jnp.where(ends, ghost_value, value))
                elif axis == 1:
                    low = pltpu.roll(inside, 32, 1)[:, :128]
                    high = pltpu.roll(inside, 224, 1)[:, 128:]
                    low = jnp.where(lane16 < 32, ghost_value, low)
                    high = jnp.where(lane16 >= 96, ghost_value, high)
                    rim.append(jnp.concatenate([low, high], axis=1))
                else:
                    low = jnp.where(row_low < 2, ghost_value, pltpu.roll(inside, 2, 0)[:8])
                    high = jnp.where(row_low >= 6, ghost_value, pltpu.roll(inside, 14, 0)[8:])
                    rim.append(jnp.concatenate([low, high], axis=0))
            change = sweep(rim, axis)
            up, down, dim = ((2, 254, 1), (32, 224, 1), (2, 14, 0))[axis]
            for k in range(5):
                edge = jnp.where(places[axis] >= 14, pltpu.roll(change[k], up, dim), 0.0)
                edge = jnp.where(places[axis] < 2, pltpu.roll(change[k], down, dim), edge)
                total[k] = total[k] + edge
        taken = new_source[base + j] >= 0
        for k in range(5):
            out[j, k] = jnp.where(taken, ratio * total[k] - box[k], 0.0)
        pltpu.make_async_copy(out.at[j], out_hbm.at[j], out_sems.at[j]).start()

    for j in range(slots):
        pltpu.make_async_copy(out.at[j], out_hbm.at[j], out_sems.at[j]).wait()


def body(sizes, fields, new_source, ghost_source):
    curves, subs = sizes
    slots = fields.shape[0]
    ghost = ghost_source.T
    f32 = jnp.float32
    tile = (5, 16, 128)
    negated = pl.pallas_call(
        functools.partial(step_kernel, sizes),
        out_shape=jax.ShapeDtypeStruct(fields.shape, f32),
        in_specs=[pl.BlockSpec(memory_space=pltpu.HBM)] * 3,
        out_specs=pl.BlockSpec(memory_space=pltpu.HBM),
        scratch_shapes=[
            pltpu.VMEM(fields.shape, f32),
            pltpu.SemaphoreType.DMA((slots,)),
            pltpu.VMEM(fields.shape, f32),
            pltpu.VMEM((5,) + tile, f32),
            pltpu.VMEM(fields.shape, f32),
            pltpu.SMEM((2, slots * 6), jnp.int32),
            pltpu.VMEM(fields.shape, f32),
            pltpu.SMEM(new_source.shape, jnp.int32),
            pltpu.SMEM(ghost.shape, jnp.int32),
            pltpu.SemaphoreType.DMA((3,)),
            pltpu.VMEM((slots * 6,) + tile, f32),
            pltpu.VMEM((2,) + fields.shape[1:], f32),
            pltpu.VMEM((2,) + fields.shape[1:], f32),
            pltpu.VMEM((4,) + tile, f32),
            pltpu.VMEM((4,) + tile, f32),
            pltpu.VMEM((8, 128), f32),
            pltpu.VMEM((subs - 1, 8, 128), f32),
            pltpu.VMEM((8, 128), f32),
            pltpu.VMEM((curves - 1, 8, 128), f32),
            pltpu.SemaphoreType.DMA((2, 2, 5)),
            pltpu.SemaphoreType.DMA((2, 4, 5)),
            pltpu.SemaphoreType.DMA((2, subs - 1)),
            pltpu.SemaphoreType.DMA((2, curves - 1)),
        ],
        compiler_params=pltpu.CompilerParams(
            collective_id=0, has_side_effects=True, vmem_limit_bytes=60 << 20
        ),
    )(fields, new_source, ghost)
    return -negated


def solution(mesh):
    placed = P(("curve", "sub"), None, None, None)
    sizes = (mesh.shape["curve"], mesh.shape["sub"])
    return jax.shard_map(
        functools.partial(body, sizes),
        mesh=mesh,
        in_specs=(placed, P(), P()),
        out_specs=placed,
        check_vma=False,
    )
```
